32 devices in a mesh: band: 4 (over x, core), fft: 8 (over z, y).
Axes of the slice: x: 2, y: 2, z: 4, core: 2. Of those that a mesh axis runs over, the one named last changes fastest.
Arguments:
- valence_waves: bfloat16 [8, 96, 96, 96], P('band', 'fft'), may hold values from -6 to 6
- conduction_waves: bfloat16 [4, 96, 96, 96], P(None, 'fft'), may hold values from -6 to 6
- valence_energy: float32 [8], P('band'), may hold values from -1 to -0.1
- conduction_energy: float32 [4], replicated, may hold values from 0.1 to 1
- sphere_slots: int32 [16384], P('fft'), may hold values from 0 to 221183, as said below
Outputs:
- static_response: float32 [16384, 16384], P('fft', 'band')
The draws below stay inside these ranges and needn't reach their ends.
Inputs may be any that keep to these rules, and one draw needn't show every extreme that they name: `sphere_slots`: entries g of one fft device's block (g // 2048 equal) are distinct; each block holds 0 and 221183.
All inputs are finite; a program needn't handle non-finite values.
Results may differ from the reference program's by a relative error of at most 0.009.
Values may be sent and summed in bfloat16 or wider, within the bound.
A program may use at most 320 MiB of HBM per device.

```python
import math
import jax
import jax.numpy as jnp
from jax import lax

GRID = 96
NG = 16384
CB = 4
NVAL = 8
YSLAB = 12
NG_DEV = 2048
PAIRS = 32


def draw_sphere_slots(key, part):
    key = jax.random.fold_in(key, 11)
    local_size = GRID * YSLAB * 2 * GRID
    groups = NG // NG_DEV

    def one_device(index):
        device_key = jax.random.fold_in(key, index)
        inner = jax.random.permutation(device_key, local_size - 2)[:NG_DEV - 2] + 1
        ends = jnp.array([0, local_size - 1], dtype=jnp.int32)
        block = jnp.concatenate([ends, inner.astype(jnp.int32)])
        order = jax.random.permutation(jax.random.fold_in(device_key, 1), NG_DEV)
        return block[order]
    return jax.vmap(one_device)(jnp.arange(groups, dtype=jnp.int32)).reshape(NG)


def level_of(own_key, extent, pieces, least, high):
    loudness = 1.0
    for axis_at, blocks in pieces:
        draws = jax.random.uniform(jax.random.fold_in(jax.random.fold_in(own_key, 6), axis_at), (blocks,), jnp.float32, least / len(pieces), high / len(pieces))
        loudness = loudness * jnp.repeat(jnp.exp(draws), extent[axis_at] // blocks).reshape((-1,) + (1,) * (len(extent) - 1 - axis_at))
    return loudness


def gaussian(own_key, extent, spread, reach, pieces=(), kind=jnp.bfloat16):
    entries = jax.random.normal(own_key, extent, jnp.float32) * spread
    if len(pieces) > 0:
        entries = level_of(own_key, extent, pieces, -0.22, 0.18) * entries
    return jnp.clip(entries, min=-reach, max=reach).astype(kind)


def setup_inputs(seed: int = 0) -> dict:
    key_of = jax.random.split(jax.random.key(seed), 6)
    valence_waves = gaussian(key_of[0], (NVAL, GRID, GRID, GRID), 1.0, 6.0, ((0, 4), (1, 8)))
    conduction_waves = gaussian(key_of[1], (CB, GRID, GRID, GRID), 1.0, 6.0, ((1, 8),))
    valence_energy = jnp.clip(-1.0 + 0.9 * jax.random.uniform(key_of[2], (NVAL,), jnp.float32) ** level_of(key_of[2], (NVAL,), ((0, 4),), -0.2, 0.2), -1.0, -0.1)
    conduction_energy = jnp.clip(jax.random.uniform(key_of[3], (CB,), jnp.float32, 0.1, 1.0), 0.1, 1.0)
    sphere_slots = draw_sphere_slots(jax.random.fold_in(key_of[5], 71), 0)
    return dict(valence_waves=valence_waves, conduction_waves=conduction_waves, valence_energy=valence_energy, conduction_energy=conduction_energy, sphere_slots=sphere_slots)


def dft_tables(length):
    counter = jnp.arange(length, dtype=jnp.int32)
    product = counter[:, None] * counter[None, :] % length
    angles = product.astype(jnp.float32) * (2.0 * math.pi / length)
    factor = 1.0 / math.sqrt(length)
    return ((jnp.cos(angles) * factor).astype(jnp.bfloat16), (jnp.sin(angles) * factor).astype(jnp.bfloat16))

def rounded(values):
    return lax.optimization_barrier(values.astype(jnp.bfloat16)).astype(jnp.float32)

def reference(valence_waves, conduction_waves, valence_energy, conduction_energy, sphere_slots):
    highest = lax.Precision.HIGHEST
    table_cos, table_sin = dft_tables(GRID)
    cos_wide = table_cos.astype(jnp.float32)
    sin_wide = table_sin.astype(jnp.float32)
    first_table = jnp.concatenate([cos_wide, -sin_wide], axis=1)
    width = 2 * GRID
    owner = jnp.arange(NG, dtype=jnp.int32) // NG_DEV
    kx_index = sphere_slots // (YSLAB * width)
    remain = sphere_slots % (YSLAB * width)
    component = remain % width
    column = owner * (YSLAB * width) + remain
    mirror = column - component + (component + GRID) % width
    signs = jnp.where(component < GRID, 1.0, -1.0).astype(jnp.float32)
    onehot = (kx_index[:, None] == jnp.arange(GRID, dtype=jnp.int32)[None, :]).astype(jnp.float32)
    coef_cos = jnp.dot(onehot, cos_wide, precision=highest)
    coef_sin = signs[:, None] * jnp.dot(onehot, sin_wide, precision=highest)

    def one_band(index):
        density = rounded(valence_waves[index][None].astype(jnp.float32) * conduction_waves.astype(jnp.float32))
        first_pass = rounded(jnp.einsum('cxyz,zk->cxyk', density, first_table, precision=highest))
        direct = jnp.einsum('ky,cxyq->cxkq', cos_wide, first_pass, precision=highest)
        swapped = jnp.einsum('ky,cxyq->cxkq', sin_wide, first_pass, precision=highest)
        real_part = direct[..., :GRID] + swapped[..., GRID:]
        imag_part = direct[..., GRID:] - swapped[..., :GRID]
        second_pass = rounded(jnp.concatenate([real_part, imag_part], axis=-1))
        flat = second_pass.reshape(CB, GRID, GRID * width)
        elements = jnp.einsum('cxg,gx->cg', flat[:, :, column], coef_cos, precision=highest)
        elements = elements + jnp.einsum('cxg,gx->cg', flat[:, :, mirror], coef_sin, precision=highest)
        spacing = conduction_energy - valence_energy[index]
        factor = jnp.sqrt(4.0 / (spacing * PAIRS))
        return (factor[:, None] * elements).astype(jnp.bfloat16)
    scaled = lax.map(one_band, jnp.arange(NVAL, dtype=jnp.int32)).reshape(NVAL * CB, NG).astype(jnp.float32)
    return -jnp.dot(scaled.T, scaled, precision=highest)
```

```python
import functools
import math

import jax
import jax.numpy as jnp
from jax import lax
from jax.experimental import pallas as pl
from jax.experimental.pallas import tpu as pltpu
from jax.sharding import PartitionSpec as P

LANES = 128


def dft_tables(length):
    counter = jnp.arange(length, dtype=jnp.int32)
    product = counter[:, None] * counter[None, :] % length
    angles = product.astype(jnp.float32) * (2.0 * math.pi / length)
    factor = 1.0 / math.sqrt(length)
    return (
        (jnp.cos(angles) * factor).astype(jnp.bfloat16),
        (jnp.sin(angles) * factor).astype(jnp.bfloat16),
    )


def transform(valence_ref, conduction_ref, first_ref, second_ref, planes, length):
    bands = conduction_ref.shape[0]
    pairs = valence_ref.shape[0] * bands
    slab = valence_ref.shape[1]

    def one_plane(x, carry):
        for v in range(valence_ref.shape[0]):
            density = (valence_ref[v, x][None] * conduction_ref[:, x]).reshape(bands * length, length)
            first = jnp.dot(density, first_ref[...], preferred_element_type=jnp.float32)
            first = first.astype(jnp.bfloat16)
            for c in range(0, bands, 2):
                columns = []
                for d in range(c, c + 2):
                    one = first[d * length : (d + 1) * length]
                    columns.append(jnp.concatenate([one[:, :LANES], one[:, LANES:]], axis=0))
                both = jnp.concatenate(columns, axis=1)
                second = jnp.dot(second_ref[...], both, preferred_element_type=jnp.float32)
                for d in range(2):
                    row = x * pairs + v * bands + c + d
                    planes[pl.ds(row, 2 * length, stride=slab * pairs), :] = second[
                        :, d * LANES : (d + 1) * LANES
                    ]
        return carry

    lax.fori_loop(0, slab, one_plane, 0)


def sample_tile(codes, left, xtable_ref, pairs, slab):
    tile = codes.shape[1]
    depth = left.shape[1]
    kx = codes & 255
    column = (codes >> 8) & 4095
    imag = (codes >> 20) > 0
    hot = lax.broadcasted_iota(jnp.int32, (depth, tile), 0) == column
    hot = jnp.where(hot, 1.0, 0.0).astype(jnp.bfloat16)
    picked = jnp.dot(left[...], hot, preferred_element_type=jnp.float32)
    hot_x = lax.broadcasted_iota(jnp.int32, (LANES, tile), 0) == kx
    hot_x = jnp.where(hot_x, 1.0, 0.0).astype(jnp.bfloat16)
    waves = jnp.dot(xtable_ref[...], hot_x, preferred_element_type=jnp.float32)
    half = waves.shape[0] // 2
    cos, sin = waves[:half], waves[half:]
    with_re = jnp.where(imag, -sin, cos)
    with_im = jnp.where(imag, cos, sin)
    total = jnp.zeros((pairs, tile), jnp.float32)
    for x in range(slab):
        re = picked[x * pairs : (x + 1) * pairs]
        im = picked[(slab + x) * pairs : (slab + x + 1) * pairs]
        total += with_re[x : x + 1] * re + with_im[x : x + 1] * im
    return total


def elements_kernel(length, owners, tile, codes_ref, valence_ref, conduction_ref, first_ref,
                    second_ref, xtable_ref, out_ref, planes, left):
    pairs = valence_ref.shape[0] * conduction_ref.shape[0]
    slab = valence_ref.shape[1]
    rows = 2 * slab * pairs
    own = codes_ref.shape[1] // owners
    yslab = length // owners
    transform(valence_ref, conduction_ref, first_ref, second_ref, planes, length)

    def one_owner(o, carry):
        for k in range(yslab):
            part = planes[pl.ds(pl.multiple_of((o * yslab + k) * rows, rows), rows), :]
            left[:, k * LANES : (k + 1) * LANES] = part.astype(jnp.bfloat16)

        def one_tile(t, carry):
            at = pl.ds(pl.multiple_of(o * own + t * tile, tile), tile)
            out_ref[:, at] = sample_tile(codes_ref[:, at], left, xtable_ref, pairs, slab)
            return carry

        return lax.fori_loop(0, own // tile, one_tile, carry)

    lax.fori_loop(0, owners, one_owner, 0)


def on_device(valence_waves, conduction_waves, valence_energy, conduction_energy, sphere_slots):
    length = conduction_waves.shape[2]
    bands = conduction_waves.shape[0]
    slab = conduction_waves.shape[1]
    groups = lax.axis_size("band")
    owners = lax.axis_size("fft")
    pairs = valence_waves.shape[0] * bands
    pairs_all = groups * pairs
    own = sphere_slots.shape[0]
    yslab = length // owners
    me = lax.axis_index("fft")

    table_cos, table_sin = dft_tables(length)
    gap = ((0, 0), (0, LANES - length))
    first_table = jnp.concatenate([jnp.pad(table_cos, gap), jnp.pad(-table_sin, gap)], axis=1)
    second_table = jnp.stack(
        [
            jnp.concatenate([table_cos, table_sin], axis=1),
            jnp.concatenate([-table_sin, table_cos], axis=1),
        ],
        axis=1,
    ).reshape(2 * length, 2 * length)
    short = -slab % 16
    pieces = []
    for table in (table_cos, table_sin):
        piece = lax.dynamic_slice_in_dim(table, me * slab, slab, axis=0)
        pieces.append(jnp.pad(piece, ((0, short), (0, LANES - length))))
    xtable = jnp.concatenate(pieces, axis=0)

    width = 2 * length
    kx = sphere_slots // (yslab * width)
    ky = (sphere_slots // width) % yslab
    comp = sphere_slots % width
    imag = (comp >= length).astype(jnp.int32)
    codes = kx + ((ky * LANES + comp - imag * length) << 8) + (imag << 20)
    codes = lax.all_gather(codes, "fft", axis=0, tiled=True)[None]

    partial = pl.pallas_call(
        functools.partial(elements_kernel, length, owners, min(512, own)),
        out_shape=jax.ShapeDtypeStruct((pairs, owners * own), jnp.float32),
        in_specs=[pl.BlockSpec(memory_space=pltpu.VMEM)] * 6,
        out_specs=pl.BlockSpec(memory_space=pltpu.VMEM),
        scratch_shapes=[
            pltpu.VMEM((2 * length * slab * pairs, LANES), jnp.float32),
            pltpu.VMEM((2 * slab * pairs, yslab * LANES), jnp.bfloat16),
        ],
        compiler_params=pltpu.CompilerParams(vmem_limit_bytes=48 * 2**20),
        name="elements",
    )(codes, valence_waves, conduction_waves, first_table, second_table, xtable)
    elements = lax.psum_scatter(partial, "fft", scatter_dimension=1, tiled=True)
    spacing = conduction_energy[None, :] - valence_energy[:, None]
    factor = jnp.sqrt(4.0 / (spacing * pairs_all)).reshape(pairs)
    scaled = (factor[:, None] * elements).astype(jnp.bfloat16)

    rows = lax.all_gather(scaled, "band", axis=0, tiled=True)
    whole = lax.all_gather(rows, "fft", axis=1, tiled=True)
    share = owners * own // groups
    owned = lax.dynamic_slice_in_dim(whole, lax.axis_index("band") * share, share, axis=1)
    contract = (((0,), (0,)), ((), ()))
    return -lax.dot_general(rows, owned, contract, preferred_element_type=jnp.float32)


def solution(mesh):
    in_specs = (P("band", "fft", None, None), P(None, "fft", None, None), P("band"), P(), P("fft"))
    out_specs = P("fft", "band")
    return jax.shard_map(
        on_device, mesh=mesh, in_specs=in_specs, out_specs=out_specs, check_vma=False
    )
```

```python
import functools
import math

import jax
import jax.numpy as jnp
from jax import lax
from jax.experimental import pallas as pl
from jax.experimental.pallas import tpu as pltpu
from jax.sharding import PartitionSpec as P

LANES = 128
MESH = pl.DeviceIdType.MESH


def dft_tables(length):
    counter = jnp.arange(length, dtype=jnp.int32)
    product = counter[:, None] * counter[None, :] % length
    angles = product.astype(jnp.float32) * (2.0 * math.pi / length)
    factor = 1.0 / math.sqrt(length)
    return (
        (jnp.cos(angles) * factor).astype(jnp.bfloat16),
        (jnp.sin(angles) * factor).astype(jnp.bfloat16),
    )


def transform(valence_ref, conduction_ref, first_ref, second_ref, planes, length):
    bands = conduction_ref.shape[0]
    pairs = valence_ref.shape[0] * bands
    slab = valence_ref.shape[1]

    def one_plane(x, carry):
        for v in range(valence_ref.shape[0]):
            density = (valence_ref[v, x][None] * conduction_ref[:, x]).reshape(bands * length, length)
            first = jnp.dot(density, first_ref[...], preferred_element_type=jnp.float32)
            first = first.astype(jnp.bfloat16)
            for c in range(0, bands, 2):
                columns = []
                for d in range(c, c + 2):
                    one = first[d * length : (d + 1) * length]
                    columns.append(jnp.concatenate([one[:, :LANES], one[:, LANES:]], axis=0))
                both = jnp.concatenate(columns, axis=1)
                second = jnp.dot(second_ref[...], both, preferred_element_type=jnp.float32)
                for d in range(2):
                    row = x * pairs + v * bands + c + d
                    planes[pl.ds(row, 2 * length, stride=slab * pairs), :] = second[
                        :, d * LANES : (d + 1) * LANES
                    ]
        return carry

    lax.fori_loop(0, slab, one_plane, 0)


def sample_tile(codes, left, xtable_ref, pairs, slab):
    tile = codes.shape[1]
    depth = left.shape[1]
    kx = codes & 255
    column = (codes >> 8) & 4095
    imag = (codes >> 20) > 0
    hot = lax.broadcasted_iota(jnp.int32, (depth, tile), 0) == column
    hot = jnp.where(hot, 1.0, 0.0).astype(jnp.bfloat16)
    picked = jnp.dot(left[...], hot, preferred_element_type=jnp.float32)
    hot_x = lax.broadcasted_iota(jnp.int32, (LANES, tile), 0) == kx
    hot_x = jnp.where(hot_x, 1.0, 0.0).astype(jnp.bfloat16)
    waves = jnp.dot(xtable_ref[...], hot_x, preferred_element_type=jnp.float32)
    half = waves.shape[0] // 2
    cos, sin = waves[:half], waves[half:]
    with_re = jnp.where(imag, -sin, cos)
    with_im = jnp.where(imag, cos, sin)
    total = jnp.zeros((pairs, tile), jnp.float32)
    for x in range(slab):
        re = picked[x * pairs : (x + 1) * pairs]
        im = picked[(slab + x) * pairs : (slab + x + 1) * pairs]
        total += with_re[x : x + 1] * re + with_im[x : x + 1] * im
    return total


def gather_kernel(length, bands_axis, owners, tile, codes_ref, factor_ref, valence_ref, conduction_ref,
                  first_ref, second_ref, xtable_ref, rows_ref, owned_ref,
                  planes, left, codes_all, partial, arrived, row_parts, owned_parts,
                  code_send, code_recv, part_send, part_recv, row_send, row_recv, own_send, own_recv):
    pairs = valence_ref.shape[0] * conduction_ref.shape[0]
    slab = valence_ref.shape[1]
    rows = 2 * slab * pairs
    own = codes_ref.shape[1]
    half = own // 2
    yslab = length // owners
    ratio = owned_parts.shape[0]
    band = lax.axis_index("band")
    me = lax.axis_index("fft")

    def around(shift):
        return lax.rem(me + shift, owners)

    def across(shift):
        return lax.rem(band + shift, bands_axis)

    barrier = pltpu.get_barrier_semaphore()

    def greet_fft(shift, carry):
        pl.semaphore_signal(barrier, inc=1, device_id=(band, around(shift)), device_id_type=MESH)
        return carry

    def greet_band(shift, carry):
        pl.semaphore_signal(barrier, inc=1, device_id=(across(shift), me), device_id_type=MESH)
        return carry

    lax.fori_loop(1, owners, greet_fft, 0)
    lax.fori_loop(1, bands_axis, greet_band, 0)
    pl.semaphore_wait(barrier, owners + bands_axis - 2)

    def code_copy(shift):
        return pltpu.make_async_remote_copy(
            src_ref=codes_ref, dst_ref=codes_all.at[shift],
            send_sem=code_send.at[shift], recv_sem=code_recv.at[shift],
            device_id=(band, around(shift)), device_id_type=MESH,
        )

    def part_copy(shift):
        return pltpu.make_async_remote_copy(
            src_ref=partial.at[shift], dst_ref=arrived.at[shift],
            send_sem=part_send.at[shift], recv_sem=part_recv.at[shift],
            device_id=(band, around(owners - shift)), device_id_type=MESH,
        )

    def row_copy(shift):
        return pltpu.make_async_remote_copy(
            src_ref=row_parts.at[band], dst_ref=row_parts.at[band],
            send_sem=row_send.at[shift], recv_sem=row_recv.at[shift],
            device_id=(across(shift), me), device_id_type=MESH,
        )

    def row_wait(shift):
        source = across(bands_axis - shift)
        return pltpu.make_async_remote_copy(
            src_ref=row_parts.at[band], dst_ref=row_parts.at[source],
            send_sem=row_send.at[shift], recv_sem=row_recv.at[shift],
            device_id=(across(shift), me), device_id_type=MESH,
        )

    def owned_copy(shift, slot):
        return pltpu.make_async_remote_copy(
            src_ref=row_parts, dst_ref=owned_parts.at[slot],
            send_sem=own_send.at[shift], recv_sem=own_recv.at[slot],
            device_id=(band, around(shift)), device_id_type=MESH,
        )

    def each(first, last, act):
        def step(i, carry):
            act(i)
            return carry

        lax.fori_loop(first, last, step, 0)

    each(1, owners, lambda s: code_copy(s).start())
    codes_all[0] = codes_ref[...]
    transform(valence_ref, conduction_ref, first_ref, second_ref, planes, length)

    def one_owner(step):
        shift = lax.rem(step, owners)
        o = lax.rem(me + owners - shift, owners)

        @pl.when(shift > 0)
        def _():
            code_copy(shift).wait_recv()

        for k in range(yslab):
            part = planes[pl.ds(pl.multiple_of((o * yslab + k) * rows, rows), rows), :]
            left[:, k * LANES : (k + 1) * LANES] = part.astype(jnp.bfloat16)

        for t in range(0, own, tile):
            codes = codes_all[shift, :, t : t + tile]
            partial[shift, :, t : t + tile] = sample_tile(codes, left, xtable_ref, pairs, slab)

        @pl.when(shift > 0)
        def _():
            part_copy(shift).start()

    each(1, owners + 1, one_owner)
    each(1, owners, lambda s: code_copy(s).wait_send())

    each(1, owners, lambda s: part_copy(s).wait_recv())
    total = partial[0]
    for s in range(1, owners):
        total += arrived[s]
    scaled = factor_ref[:, :1] * total
    row_parts[band] = jnp.concatenate([scaled[:, :half], scaled[:, half:]], axis=0).astype(jnp.bfloat16)
    each(1, bands_axis, lambda s: row_copy(s).start())
    each(1, bands_axis, lambda s: row_wait(s).wait_recv())

    mine = me // ratio == band
    slot = lax.rem(me, ratio)

    @pl.when(mine)
    def _():
        each(1, owners, lambda s: owned_copy(s, slot).start())
        owned_parts[slot] = row_parts[...]

    def join(parts):
        parts = parts.astype(jnp.float32)
        halves = [parts[:, h * pairs : (h + 1) * pairs].reshape(bands_axis * pairs, half) for h in range(2)]
        return jnp.concatenate(halves, axis=1)

    rows_ref[...] = join(row_parts[...]).astype(jnp.bfloat16)
    for j in range(ratio):

        @pl.when(band * ratio + j != me)
        def _():
            owned_copy(1, j).wait_recv()

        owned_ref[:, j * own : (j + 1) * own] = (-join(owned_parts[j])).astype(jnp.bfloat16)

    each(1, owners, lambda s: part_copy(s).wait_send())
    each(1, bands_axis, lambda s: row_copy(s).wait_send())

    @pl.when(mine)
    def _():
        each(1, owners, lambda s: owned_copy(s, slot).wait_send())


def product_kernel(rows_ref, owned_ref, out_ref):
    contract = (((0,), (0,)), ((), ()))
    out_ref[...] = lax.dot_general(
        rows_ref[...], owned_ref[...], contract, preferred_element_type=jnp.float32
    )


def on_device(valence_waves, conduction_waves, valence_energy, conduction_energy, sphere_slots):
    length = conduction_waves.shape[2]
    bands = conduction_waves.shape[0]
    slab = conduction_waves.shape[1]
    groups = lax.axis_size("band")
    owners = lax.axis_size("fft")
    pairs = valence_waves.shape[0] * bands
    pairs_all = groups * pairs
    own = sphere_slots.shape[0]
    yslab = length // owners
    ratio = owners // groups
    me = lax.axis_index("fft")

    table_cos, table_sin = dft_tables(length)
    gap = ((0, 0), (0, LANES - length))
    first_table = jnp.concatenate([jnp.pad(table_cos, gap), jnp.pad(-table_sin, gap)], axis=1)
    second_table = jnp.stack(
        [
            jnp.concatenate([table_cos, table_sin], axis=1),
            jnp.concatenate([-table_sin, table_cos], axis=1),
        ],
        axis=1,
    ).reshape(2 * length, 2 * length)
    short = -slab % 16
    pieces = []
    for table in (table_cos, table_sin):
        piece = lax.dynamic_slice_in_dim(table, me * slab, slab, axis=0)
        pieces.append(jnp.pad(piece, ((0, short), (0, LANES - length))))
    xtable = jnp.concatenate(pieces, axis=0)

    width = 2 * length
    kx = sphere_slots // (yslab * width)
    ky = (sphere_slots // width) % yslab
    comp = sphere_slots % width
    imag = (comp >= length).astype(jnp.int32)
    codes = (kx + ((ky * LANES + comp - imag * length) << 8) + (imag << 20))[None]
    spacing = conduction_energy[None, :] - valence_energy[:, None]
    factor = jnp.sqrt(4.0 / (spacing * pairs_all)).reshape(pairs)
    factor = jnp.broadcast_to(factor[:, None], (pairs, LANES))

    rows, owned = pl.pallas_call(
        functools.partial(gather_kernel, length, groups, owners, min(512, own)),
        out_shape=(
            jax.ShapeDtypeStruct((pairs_all, own), jnp.bfloat16),
            jax.ShapeDtypeStruct((pairs_all, ratio * own), jnp.bfloat16),
        ),
        in_specs=[pl.BlockSpec(memory_space=pltpu.VMEM)] * 7,
        out_specs=(pl.BlockSpec(memory_space=pltpu.VMEM), pl.BlockSpec(memory_space=pltpu.VMEM)),
        scratch_shapes=[
            pltpu.VMEM((2 * length * slab * pairs, LANES), jnp.float32),
            pltpu.VMEM((2 * slab * pairs, yslab * LANES), jnp.bfloat16),
            pltpu.VMEM((owners, 1, own), jnp.int32),
            pltpu.VMEM((owners, pairs, own), jnp.float32),
            pltpu.VMEM((owners, pairs, own), jnp.float32),
            pltpu.VMEM((groups, 2 * pairs, own // 2), jnp.bfloat16),
            pltpu.VMEM((ratio, groups, 2 * pairs, own // 2), jnp.bfloat16),
            pltpu.SemaphoreType.DMA((owners,)),
            pltpu.SemaphoreType.DMA((owners,)),
            pltpu.SemaphoreType.DMA((owners,)),
            pltpu.SemaphoreType.DMA((owners,)),
            pltpu.SemaphoreType.DMA((groups,)),
            pltpu.SemaphoreType.DMA((groups,)),
            pltpu.SemaphoreType.DMA((owners,)),
            pltpu.SemaphoreType.DMA((ratio,)),
        ],
        compiler_params=pltpu.CompilerParams(
            collective_id=0, has_side_effects=True, vmem_limit_bytes=48 * 2**20
        ),
        name="gather",
    )(codes, factor, valence_waves, conduction_waves, first_table, second_table, xtable)

    tile = min(256, own)
    return pl.pallas_call(
        product_kernel,
        grid=(own // tile,),
        out_shape=jax.ShapeDtypeStruct((own, ratio * own), jnp.float32),
        in_specs=[
            pl.BlockSpec((pairs_all, tile), lambda i: (0, i)),
            pl.BlockSpec((pairs_all, ratio * own), lambda i: (0, 0)),
        ],
        out_specs=pl.BlockSpec((tile, ratio * own), lambda i: (i, 0)),
        compiler_params=pltpu.CompilerParams(vmem_limit_bytes=48 * 2**20),
        name="product",
    )(rows, owned)


def solution(mesh):
    in_specs = (P("band", "fft", None, None), P(None, "fft", None, None), P("band"), P(), P("fft"))
    out_specs = P("fft", "band")
    return jax.shard_map(
        on_device, mesh=mesh, in_specs=in_specs, out_specs=out_specs, check_vma=False
    )
```

```python
import functools
import math

import jax
import jax.numpy as jnp
from jax import lax
from jax.experimental import pallas as pl
from jax.experimental.pallas import tpu as pltpu
from jax.sharding import PartitionSpec as P

LANES = 128
MESH = pl.DeviceIdType.MESH


def dft_tables(length):
    counter = jnp.arange(length, dtype=jnp.int32)
    product = counter[:, None] * counter[None, :] % length
    angles = product.astype(jnp.float32) * (2.0 * math.pi / length)
    factor = 1.0 / math.sqrt(length)
    return (
        (jnp.cos(angles) * factor).astype(jnp.bfloat16),
        (jnp.sin(angles) * factor).astype(jnp.bfloat16),
    )


def transform(valence_ref, conduction_ref, first_ref, second_ref, planes, length):
    bands = conduction_ref.shape[0]
    pairs = valence_ref.shape[0] * bands
    slab = valence_ref.shape[1]

    def one_plane(x, carry):
        for v in range(valence_ref.shape[0]):
            density = (valence_ref[v, x][None] * conduction_ref[:, x]).reshape(bands * length, length)
            first = jnp.dot(density, first_ref[...], preferred_element_type=jnp.float32)
            first = first.astype(jnp.bfloat16)
            for c in range(0, bands, 2):
                columns = []
                for d in range(c, c + 2):
                    one = first[d * length : (d + 1) * length]
                    columns.append(jnp.concatenate([one[:, :LANES], one[:, LANES:]], axis=0))
                both = jnp.concatenate(columns, axis=1)
                second = jnp.dot(second_ref[...], both, preferred_element_type=jnp.float32)
                for d in range(2):
                    row = x * pairs + v * bands + c + d
                    planes[pl.ds(row, 2 * length, stride=slab * pairs), :] = second[
                        :, d * LANES : (d + 1) * LANES
                    ]
        return carry

    lax.fori_loop(0, slab, one_plane, 0)


def sample_tile(codes, left, xtable_ref, pairs, slab):
    tile = codes.shape[1]
    depth = left.shape[1]
    kx = codes & 255
    column = (codes >> 8) & 4095
    imag = (codes >> 20) > 0
    hot = lax.broadcasted_iota(jnp.int32, (depth, tile), 0) == column
    hot = jnp.where(hot, 1.0, 0.0).astype(jnp.bfloat16)
    picked = jnp.dot(left[...], hot, preferred_element_type=jnp.float32)
    hot_x = lax.broadcasted_iota(jnp.int32, (LANES, tile), 0) == kx
    hot_x = jnp.where(hot_x, 1.0, 0.0).astype(jnp.bfloat16)
    waves = jnp.dot(xtable_ref[...], hot_x, preferred_element_type=jnp.float32)
    half = waves.shape[0] // 2
    cos, sin = waves[:half], waves[half:]
    with_re = jnp.where(imag, -sin, cos)
    with_im = jnp.where(imag, cos, sin)
    total = jnp.zeros((pairs, tile), jnp.float32)
    for x in range(slab):
        re = picked[x * pairs : (x + 1) * pairs]
        im = picked[(slab + x) * pairs : (slab + x + 1) * pairs]
        total += with_re[x : x + 1] * re + with_im[x : x + 1] * im
    return total


def gather_kernel(length, bands_axis, owners, tile, codes_ref, valence_energy, conduction_energy,
                  valence_hbm, conduction_hbm, first_ref, second_ref, xtable_ref, rows_ref, owned_ref,
                  valence_ref, conduction_ref, planes, left, codes_all, work, partial, arrived,
                  row_parts, owned_parts, load_sem,
                  code_send, code_recv, part_send, part_recv, row_send, row_recv, own_send, own_recv,
                  side_send, side_recv):
    pairs = valence_ref.shape[0] * conduction_ref.shape[0]
    slab = valence_ref.shape[1]
    rows = 2 * slab * pairs
    own = codes_ref.shape[1]
    half = own // 2
    yslab = length // owners
    ratio = owned_parts.shape[0]
    band = lax.axis_index("band")
    me = lax.axis_index("fft")
    root = me // ratio
    slot = lax.rem(me, ratio)
    loads = [
        pltpu.make_async_copy(valence_hbm, valence_ref, load_sem.at[0]),
        pltpu.make_async_copy(conduction_hbm, conduction_ref, load_sem.at[1]),
    ]
    for load in loads:
        load.start()

    def around(shift):
        return lax.rem(me + shift, owners)

    def across(shift):
        return lax.rem(band + shift, bands_axis)

    barrier = pltpu.get_barrier_semaphore()

    def greet_fft(shift, carry):
        pl.semaphore_signal(barrier, inc=1, device_id=(band, around(shift)), device_id_type=MESH)
        return carry

    def greet_band(shift, carry):
        pl.semaphore_signal(barrier, inc=1, device_id=(across(shift), me), device_id_type=MESH)
        return carry

    lax.fori_loop(1, owners, greet_fft, 0)
    lax.fori_loop(1, bands_axis, greet_band, 0)
    pl.semaphore_wait(barrier, owners + bands_axis - 2)

    def code_copy(shift):
        return pltpu.make_async_remote_copy(
            src_ref=codes_ref, dst_ref=codes_all.at[shift],
            send_sem=code_send.at[shift], recv_sem=code_recv.at[shift],
            device_id=(band, around(shift)), device_id_type=MESH,
        )

    def part_copy(shift):
        return pltpu.make_async_remote_copy(
            src_ref=partial.at[shift], dst_ref=arrived.at[shift],
            send_sem=part_send.at[shift], recv_sem=part_recv.at[shift],
            device_id=(band, around(owners - shift)), device_id_type=MESH,
        )

    def row_copy(shift):
        return pltpu.make_async_remote_copy(
            src_ref=row_parts.at[band], dst_ref=row_parts.at[band],
            send_sem=row_send.at[shift], recv_sem=row_recv.at[shift],
            device_id=(across(shift), me), device_id_type=MESH,
        )

    def row_wait(shift):
        source = across(bands_axis - shift)
        return pltpu.make_async_remote_copy(
            src_ref=row_parts.at[band], dst_ref=row_parts.at[source],
            send_sem=row_send.at[shift], recv_sem=row_recv.at[shift],
            device_id=(across(shift), me), device_id_type=MESH,
        )

    def owned_copy(hop, shift):
        chunk = across(bands_axis - shift)
        return pltpu.make_async_remote_copy(
            src_ref=owned_parts.at[slot, chunk], dst_ref=owned_parts.at[slot, chunk],
            send_sem=own_send.at[hop, shift], recv_sem=own_recv.at[shift],
            device_id=(band, across(hop) * ratio + slot), device_id_type=MESH,
        )

    def side_copy(hop, shift, source):
        chunk = across(bands_axis - shift)
        return pltpu.make_async_remote_copy(
            src_ref=owned_parts.at[source, chunk], dst_ref=owned_parts.at[source, chunk],
            send_sem=side_send.at[hop, shift], recv_sem=side_recv.at[hop, shift],
            device_id=(band, root * ratio + lax.rem(slot + hop, ratio)), device_id_type=MESH,
        )

    def each(first, last, act):
        def step(i, carry):
            act(i)
            return carry

        lax.fori_loop(first, last, step, 0)

    each(1, owners, lambda s: code_copy(s).start())
    codes_all[0] = codes_ref[...]
    for load in loads:
        load.wait()
    transform(valence_ref, conduction_ref, first_ref, second_ref, planes, length)

    def folded(array):
        return jnp.concatenate([array[:, :half], array[:, half:]], axis=0)

    def one_owner(step):
        shift = lax.rem(step, owners)
        o = lax.rem(me + owners - shift, owners)

        @pl.when(shift > 0)
        def _():
            code_copy(shift).wait_recv()

        for k in range(yslab):
            part = planes[pl.ds(pl.multiple_of((o * yslab + k) * rows, rows), rows), :]
            left[:, k * LANES : (k + 1) * LANES] = part.astype(jnp.bfloat16)

        for t in range(0, own, tile):
            codes = codes_all[shift, :, t : t + tile]
            work[:, t : t + tile] = sample_tile(codes, left, xtable_ref, pairs, slab)

        @pl.when(shift > 0)
        def _():
            partial[shift] = folded(work).astype(jnp.bfloat16)
            part_copy(shift).start()

    each(1, owners + 1, one_owner)
    each(1, owners, lambda s: code_copy(s).wait_send())

    line = lax.broadcasted_iota(jnp.int32, (2 * pairs, LANES), 0)
    spacing = jnp.ones((2 * pairs, LANES), jnp.float32)
    bands = conduction_ref.shape[0]
    for p in range(2 * pairs):
        v, c = p % pairs // bands, p % bands
        spacing = jnp.where(line == p, conduction_energy[c] - valence_energy[v], spacing)
    factor = jnp.sqrt(4.0 / (spacing * (bands_axis * pairs)))

    total = folded(work)
    for s in range(1, owners):
        part_copy(s).wait_recv()
        total += arrived[s].astype(jnp.float32)
    row_parts[band] = (factor[:, :1] * total).astype(jnp.bfloat16)
    each(1, bands_axis, lambda s: row_copy(s).start())
    mine = root == band

    def one_chunk(shift):
        chunk = across(bands_axis - shift)

        @pl.when(shift > 0)
        def _():
            row_wait(shift).wait_recv()

        @pl.when(mine)
        def _():
            owned_parts[slot, chunk] = row_parts[chunk]
            each(1, bands_axis, lambda hop: owned_copy(hop, shift).start())

        @pl.when(jnp.logical_not(mine))
        def _():
            owned_copy(0, shift).wait_recv()

        for hop in range(1, ratio):
            side_copy(hop, shift, slot).start()

    each(0, bands_axis, one_chunk)

    def join(parts):
        parts = parts.astype(jnp.float32)
        halves = [parts[:, h * pairs : (h + 1) * pairs].reshape(bands_axis * pairs, half) for h in range(2)]
        return jnp.concatenate(halves, axis=1)

    rows_ref[...] = join(row_parts[...]).astype(jnp.bfloat16)
    for hop in range(1, ratio):
        source = lax.rem(slot + ratio - hop, ratio)
        each(0, bands_axis, lambda s: side_copy(hop, s, source).wait_recv())
    for j in range(ratio):
        owned_ref[:, j * own : (j + 1) * own] = (-join(owned_parts[j])).astype(jnp.bfloat16)

    each(1, owners, lambda s: part_copy(s).wait_send())
    each(1, bands_axis, lambda s: row_copy(s).wait_send())

    @pl.when(mine)
    def _():
        each(0, bands_axis, lambda s: each(1, bands_axis, lambda hop: owned_copy(hop, s).wait_send()))

    for hop in range(1, ratio):
        each(0, bands_axis, lambda s: side_copy(hop, s, slot).wait_send())


def product_kernel(rows_ref, owned_ref, out_ref):
    contract = (((0,), (0,)), ((), ()))
    out_ref[...] = lax.dot_general(
        rows_ref[...], owned_ref[...], contract, preferred_element_type=jnp.float32
    )


def on_device(valence_waves, conduction_waves, valence_energy, conduction_energy, sphere_slots):
    length = conduction_waves.shape[2]
    bands = conduction_waves.shape[0]
    slab = conduction_waves.shape[1]
    groups = lax.axis_size("band")
    owners = lax.axis_size("fft")
    pairs = valence_waves.shape[0] * bands
    pairs_all = groups * pairs
    own = sphere_slots.shape[0]
    yslab = length // owners
    ratio = owners // groups
    me = lax.axis_index("fft")

    table_cos, table_sin = dft_tables(length)
    gap = ((0, 0), (0, LANES - length))
    first_table = jnp.concatenate([jnp.pad(table_cos, gap), jnp.pad(-table_sin, gap)], axis=1)
    second_table = jnp.stack(
        [
            jnp.concatenate([table_cos, table_sin], axis=1),
            jnp.concatenate([-table_sin, table_cos], axis=1),
        ],
        axis=1,
    ).reshape(2 * length, 2 * length)
    short = -slab % 16
    pieces = []
    for table in (table_cos, table_sin):
        piece = lax.dynamic_slice_in_dim(table, me * slab, slab, axis=0)
        pieces.append(jnp.pad(piece, ((0, short), (0, LANES - length))))
    xtable = jnp.concatenate(pieces, axis=0)

    width = 2 * length
    kx = sphere_slots // (yslab * width)
    ky = (sphere_slots // width) % yslab
    comp = sphere_slots % width
    imag = (comp >= length).astype(jnp.int32)
    codes = (kx + ((ky * LANES + comp - imag * length) << 8) + (imag << 20))[None]
    rows, owned = pl.pallas_call(
        functools.partial(gather_kernel, length, groups, owners, min(512, own)),
        out_shape=(
            jax.ShapeDtypeStruct((pairs_all, own), jnp.bfloat16),
            jax.ShapeDtypeStruct((pairs_all, ratio * own), jnp.bfloat16),
        ),
        in_specs=[pl.BlockSpec(memory_space=pltpu.VMEM)]
        + [pl.BlockSpec(memory_space=pltpu.SMEM)] * 2
        + [pl.BlockSpec(memory_space=pl.ANY)] * 2
        + [pl.BlockSpec(memory_space=pltpu.VMEM)] * 3,
        out_specs=(pl.BlockSpec(memory_space=pltpu.VMEM), pl.BlockSpec(memory_space=pltpu.VMEM)),
        scratch_shapes=[
            pltpu.VMEM(valence_waves.shape, jnp.bfloat16),
            pltpu.VMEM(conduction_waves.shape, jnp.bfloat16),
            pltpu.VMEM((2 * length * slab * pairs, LANES), jnp.float32),
            pltpu.VMEM((2 * slab * pairs, yslab * LANES), jnp.bfloat16),
            pltpu.VMEM((owners, 1, own), jnp.int32),
            pltpu.VMEM((pairs, own), jnp.float32),
            pltpu.VMEM((owners, 2 * pairs, own // 2), jnp.bfloat16),
            pltpu.VMEM((owners, 2 * pairs, own // 2), jnp.bfloat16),
            pltpu.VMEM((groups, 2 * pairs, own // 2), jnp.bfloat16),
            pltpu.VMEM((ratio, groups, 2 * pairs, own // 2), jnp.bfloat16),
            pltpu.SemaphoreType.DMA((2,)),
            pltpu.SemaphoreType.DMA((owners,)),
            pltpu.SemaphoreType.DMA((owners,)),
            pltpu.SemaphoreType.DMA((owners,)),
            pltpu.SemaphoreType.DMA((owners,)),
            pltpu.SemaphoreType.DMA((groups,)),
            pltpu.SemaphoreType.DMA((groups,)),
            pltpu.SemaphoreType.DMA((groups, groups)),
            pltpu.SemaphoreType.DMA((groups,)),
            pltpu.SemaphoreType.DMA((ratio, groups)),
            pltpu.SemaphoreType.DMA((ratio, groups)),
        ],
        compiler_params=pltpu.CompilerParams(
            collective_id=0, has_side_effects=True, vmem_limit_bytes=48 * 2**20
        ),
        name="gather",
    )(codes, valence_energy, conduction_energy, valence_waves, conduction_waves, first_table, second_table, xtable)

    tile = min(128, own)
    return pl.pallas_call(
        product_kernel,
        grid=(own // tile,),
        out_shape=jax.ShapeDtypeStruct((own, ratio * own), jnp.float32),
        in_specs=[
            pl.BlockSpec((pairs_all, tile), lambda i: (0, i)),
            pl.BlockSpec((pairs_all, ratio * own), lambda i: (0, 0)),
        ],
        out_specs=pl.BlockSpec((tile, ratio * own), lambda i: (i, 0)),
        compiler_params=pltpu.CompilerParams(vmem_limit_bytes=48 * 2**20),
        name="product",
    )(rows, owned)


def solution(mesh):
    in_specs = (P("band", "fft", None, None), P(None, "fft", None, None), P("band"), P(), P("fft"))
    out_specs = P("fft", "band")
    return jax.shard_map(
        on_device, mesh=mesh, in_specs=in_specs, out_specs=out_specs, check_vma=False
    )
```

```python
import functools
import math

import jax
import jax.numpy as jnp
from jax import lax
from jax.experimental import pallas as pl
from jax.experimental.pallas import tpu as pltpu
from jax.sharding import PartitionSpec as P

LANES = 128
MESH = pl.DeviceIdType.MESH


def dft_tables(length):
    counter = jnp.arange(length, dtype=jnp.int32)
    product = counter[:, None] * counter[None, :] % length
    angles = product.astype(jnp.float32) * (2.0 * math.pi / length)
    factor = 1.0 / math.sqrt(length)
    return (
        (jnp.cos(angles) * factor).astype(jnp.bfloat16),
        (jnp.sin(angles) * factor).astype(jnp.bfloat16),
    )


def transform(valence_ref, conduction_ref, first_ref, second_ref, planes, length):
    bands = conduction_ref.shape[0]
    pairs = valence_ref.shape[0] * bands
    slab = valence_ref.shape[1]

    def one_plane(x, carry):
        for v in range(valence_ref.shape[0]):
            density = (valence_ref[v, x][None] * conduction_ref[:, x]).reshape(bands * length, length)
            first = jnp.dot(density, first_ref[...], preferred_element_type=jnp.float32)
            first = first.astype(jnp.bfloat16)
            for c in range(0, bands, 2):
                columns = []
                for d in range(c, c + 2):
                    one = first[d * length : (d + 1) * length]
                    columns.append(jnp.concatenate([one[:, :LANES], one[:, LANES:]], axis=0))
                both = jnp.concatenate(columns, axis=1)
                second = jnp.dot(second_ref[...], both, preferred_element_type=jnp.float32)
                for d in range(2):
                    row = x * pairs + v * bands + c + d
                    planes[pl.ds(row, 2 * length, stride=slab * pairs), :] = second[
                        :, d * LANES : (d + 1) * LANES
                    ]
        return carry

    lax.fori_loop(0, slab, one_plane, 0)


def sample_tile(codes, left, xtable_ref, pairs, slab):
    tile = codes.shape[1]
    depth = left.shape[1]
    kx = codes & 255
    q = (codes >> 8) & (LANES - 1)
    ky = (codes >> 15) & 31
    imag = (codes >> 20) > 0
    hot_q = lax.broadcasted_iota(jnp.int32, (LANES, tile), 0) == q
    hot_q = jnp.where(hot_q, 1.0, 0.0).astype(jnp.bfloat16)
    blocks = []
    for k in range(depth // LANES):
        blocks.append(hot_q * jnp.where(ky == k, 1.0, 0.0).astype(jnp.bfloat16))
    hot = jnp.concatenate(blocks, axis=0)
    picked = jnp.dot(left[...], hot, preferred_element_type=jnp.float32)
    hot_x = lax.broadcasted_iota(jnp.int32, (LANES, tile), 0) == kx
    hot_x = jnp.where(hot_x, 1.0, 0.0).astype(jnp.bfloat16)
    waves = jnp.dot(xtable_ref[...], hot_x, preferred_element_type=jnp.float32)
    half = waves.shape[0] // 2
    cos, sin = waves[:half], waves[half:]
    with_re = jnp.where(imag, -sin, cos)
    with_im = jnp.where(imag, cos, sin)
    total = jnp.zeros((pairs, tile), jnp.float32)
    for x in range(slab):
        re = picked[x * pairs : (x + 1) * pairs]
        im = picked[(slab + x) * pairs : (slab + x + 1) * pairs]
        total += with_re[x : x + 1] * re + with_im[x : x + 1] * im
    return total


def gather_kernel(length, bands_axis, owners, tile, codes_ref, valence_energy, conduction_energy,
                  valence_hbm, conduction_hbm, first_ref, second_ref, xtable_ref, rows_ref, owned_ref,
                  valence_ref, conduction_ref, planes, left, codes_all, work, partial, arrived,
                  row_parts, owned_parts, load_sem,
                  code_send, code_recv, part_send, part_recv, row_send, row_recv, own_send, own_recv,
                  side_send, side_recv):
    pairs = valence_ref.shape[0] * conduction_ref.shape[0]
    slab = valence_ref.shape[1]
    rows = 2 * slab * pairs
    own = codes_ref.shape[1]
    half = own // 2
    yslab = length // owners
    ratio = owned_parts.shape[0]
    band = lax.axis_index("band")
    me = lax.axis_index("fft")
    root = me // ratio
    slot = lax.rem(me, ratio)
    loads = [
        pltpu.make_async_copy(valence_hbm, valence_ref, load_sem.at[0]),
        pltpu.make_async_copy(conduction_hbm, conduction_ref, load_sem.at[1]),
    ]
    for load in loads:
        load.start()

    def around(shift):
        return lax.rem(me + shift, owners)

    def across(shift):
        return lax.rem(band + shift, bands_axis)

    barrier = pltpu.get_barrier_semaphore()

    def greet_fft(shift, carry):
        pl.semaphore_signal(barrier, inc=1, device_id=(band, around(shift)), device_id_type=MESH)
        return carry

    def greet_band(shift, carry):
        pl.semaphore_signal(barrier, inc=1, device_id=(across(shift), me), device_id_type=MESH)
        return carry

    lax.fori_loop(1, owners, greet_fft, 0)
    lax.fori_loop(1, bands_axis, greet_band, 0)
    pl.semaphore_wait(barrier, owners + bands_axis - 2)

    def code_copy(shift):
        return pltpu.make_async_remote_copy(
            src_ref=codes_ref, dst_ref=codes_all.at[shift],
            send_sem=code_send.at[shift], recv_sem=code_recv.at[shift],
            device_id=(band, around(shift)), device_id_type=MESH,
        )

    def part_copy(shift):
        return pltpu.make_async_remote_copy(
            src_ref=partial.at[shift], dst_ref=arrived.at[shift],
            send_sem=part_send.at[shift], recv_sem=part_recv.at[shift],
            device_id=(band, around(owners - shift)), device_id_type=MESH,
        )

    def row_copy(shift):
        return pltpu.make_async_remote_copy(
            src_ref=row_parts.at[band], dst_ref=row_parts.at[band],
            send_sem=row_send.at[shift], recv_sem=row_recv.at[shift],
            device_id=(across(shift), me), device_id_type=MESH,
        )

    def row_wait(shift):
        source = across(bands_axis - shift)
        return pltpu.make_async_remote_copy(
            src_ref=row_parts.at[band], dst_ref=row_parts.at[source],
            send_sem=row_send.at[shift], recv_sem=row_recv.at[shift],
            device_id=(across(shift), me), device_id_type=MESH,
        )

    def owned_copy(hop, shift):
        chunk = across(bands_axis - shift)
        return pltpu.make_async_remote_copy(
            src_ref=owned_parts.at[slot, chunk], dst_ref=owned_parts.at[slot, chunk],
            send_sem=own_send.at[hop, shift], recv_sem=own_recv.at[shift],
            device_id=(band, across(hop) * ratio + slot), device_id_type=MESH,
        )

    def side_copy(hop, shift, source):
        chunk = across(bands_axis - shift)
        return pltpu.make_async_remote_copy(
            src_ref=owned_parts.at[source, chunk], dst_ref=owned_parts.at[source, chunk],
            send_sem=side_send.at[hop, shift], recv_sem=side_recv.at[hop, shift],
            device_id=(band, root * ratio + lax.rem(slot + hop, ratio)), device_id_type=MESH,
        )

    def each(first, last, act):
        def step(i, carry):
            act(i)
            return carry

        lax.fori_loop(first, last, step, 0)

    each(1, owners, lambda s: code_copy(s).start())
    codes_all[0] = codes_ref[...]
    for load in loads:
        load.wait()
    transform(valence_ref, conduction_ref, first_ref, second_ref, planes, length)

    def folded(array):
        return jnp.concatenate([array[:, :half], array[:, half:]], axis=0)

    def one_owner(step):
        shift = lax.rem(step, owners)
        o = lax.rem(me + owners - shift, owners)

        @pl.when(shift > 0)
        def _():
            code_copy(shift).wait_recv()

        for k in range(yslab):
            part = planes[pl.ds(pl.multiple_of((o * yslab + k) * rows, rows), rows), :]
            left[:, k * LANES : (k + 1) * LANES] = part.astype(jnp.bfloat16)

        for t in range(0, own, tile):
            codes = codes_all[shift, :, t : t + tile]
            work[:, t : t + tile] = sample_tile(codes, left, xtable_ref, pairs, slab)

        @pl.when(shift > 0)
        def _():
            partial[shift] = folded(work).astype(jnp.bfloat16)
            part_copy(shift).start()

    each(1, owners + 1, one_owner)
    each(1, owners, lambda s: code_copy(s).wait_send())

    line = lax.broadcasted_iota(jnp.int32, (2 * pairs, LANES), 0)
    spacing = jnp.ones((2 * pairs, LANES), jnp.float32)
    bands = conduction_ref.shape[0]
    for p in range(2 * pairs):
        v, c = p % pairs // bands, p % bands
        spacing = jnp.where(line == p, conduction_energy[c] - valence_energy[v], spacing)
    factor = jnp.sqrt(4.0 / (spacing * (bands_axis * pairs)))

    total = folded(work)
    for s in range(1, owners):
        part_copy(s).wait_recv()
        total += arrived[s].astype(jnp.float32)
    row_parts[band] = (factor[:, :1] * total).astype(jnp.bfloat16)
    each(1, bands_axis, lambda s: row_copy(s).start())
    mine = root == band

    def one_chunk(shift):
        chunk = across(bands_axis - shift)

        @pl.when(shift > 0)
        def _():
            row_wait(shift).wait_recv()

        @pl.when(mine)
        def _():
            owned_parts[slot, chunk] = row_parts[chunk]
            each(1, bands_axis, lambda hop: owned_copy(hop, shift).start())

        @pl.when(jnp.logical_not(mine))
        def _():
            owned_copy(0, shift).wait_recv()

        for hop in range(1, ratio):
            side_copy(hop, shift, slot).start()

    each(0, bands_axis, one_chunk)

    def join(parts):
        parts = parts.astype(jnp.float32)
        halves = [parts[:, h * pairs : (h + 1) * pairs].reshape(bands_axis * pairs, half) for h in range(2)]
        return jnp.concatenate(halves, axis=1)

    rows_ref[...] = join(row_parts[...]).astype(jnp.bfloat16)
    for hop in range(1, ratio):
        source = lax.rem(slot + ratio - hop, ratio)
        each(0, bands_axis, lambda s: side_copy(hop, s, source).wait_recv())
    for j in range(ratio):
        owned_ref[:, j * own : (j + 1) * own] = (-join(owned_parts[j])).astype(jnp.bfloat16)

    each(1, owners, lambda s: part_copy(s).wait_send())
    each(1, bands_axis, lambda s: row_copy(s).wait_send())

    @pl.when(mine)
    def _():
        each(0, bands_axis, lambda s: each(1, bands_axis, lambda hop: owned_copy(hop, s).wait_send()))

    for hop in range(1, ratio):
        each(0, bands_axis, lambda s: side_copy(hop, s, slot).wait_send())


def product_kernel(rows_ref, owned_ref, out_ref):
    contract = (((0,), (0,)), ((), ()))
    out_ref[...] = lax.dot_general(
        rows_ref[...], owned_ref[...], contract, preferred_element_type=jnp.float32
    )


def on_device(valence_waves, conduction_waves, valence_energy, conduction_energy, sphere_slots):
    length = conduction_waves.shape[2]
    bands = conduction_waves.shape[0]
    slab = conduction_waves.shape[1]
    groups = lax.axis_size("band")
    owners = lax.axis_size("fft")
    pairs = valence_waves.shape[0] * bands
    pairs_all = groups * pairs
    own = sphere_slots.shape[0]
    yslab = length // owners
    ratio = owners // groups
    me = lax.axis_index("fft")

    table_cos, table_sin = dft_tables(length)
    gap = ((0, 0), (0, LANES - length))
    first_table = jnp.concatenate([jnp.pad(table_cos, gap), jnp.pad(-table_sin, gap)], axis=1)
    second_table = jnp.stack(
        [
            jnp.concatenate([table_cos, table_sin], axis=1),
            jnp.concatenate([-table_sin, table_cos], axis=1),
        ],
        axis=1,
    ).reshape(2 * length, 2 * length)
    short = -slab % 16
    pieces = []
    for table in (table_cos, table_sin):
        piece = lax.dynamic_slice_in_dim(table, me * slab, slab, axis=0)
        pieces.append(jnp.pad(piece, ((0, short), (0, LANES - length))))
    xtable = jnp.concatenate(pieces, axis=0)

    width = 2 * length
    kx = sphere_slots // (yslab * width)
    ky = (sphere_slots // width) % yslab
    comp = sphere_slots % width
    imag = (comp >= length).astype(jnp.int32)
    codes = (kx + ((ky * LANES + comp - imag * length) << 8) + (imag << 20))[None]
    rows, owned = pl.pallas_call(
        functools.partial(gather_kernel, length, groups, owners, min(512, own)),
        out_shape=(
            jax.ShapeDtypeStruct((pairs_all, own), jnp.bfloat16),
            jax.ShapeDtypeStruct((pairs_all, ratio * own), jnp.bfloat16),
        ),
        in_specs=[pl.BlockSpec(memory_space=pltpu.VMEM)]
        + [pl.BlockSpec(memory_space=pltpu.SMEM)] * 2
        + [pl.BlockSpec(memory_space=pl.ANY)] * 2
        + [pl.BlockSpec(memory_space=pltpu.VMEM)] * 3,
        out_specs=(pl.BlockSpec(memory_space=pltpu.VMEM), pl.BlockSpec(memory_space=pltpu.VMEM)),
        scratch_shapes=[
            pltpu.VMEM(valence_waves.shape, jnp.bfloat16),
            pltpu.VMEM(conduction_waves.shape, jnp.bfloat16),
            pltpu.VMEM((2 * length * slab * pairs, LANES), jnp.float32),
            pltpu.VMEM((2 * slab * pairs, yslab * LANES), jnp.bfloat16),
            pltpu.VMEM((owners, 1, own), jnp.int32),
            pltpu.VMEM((pairs, own), jnp.float32),
            pltpu.VMEM((owners, 2 * pairs, own // 2), jnp.bfloat16),
            pltpu.VMEM((owners, 2 * pairs, own // 2), jnp.bfloat16),
            pltpu.VMEM((groups, 2 * pairs, own // 2), jnp.bfloat16),
            pltpu.VMEM((ratio, groups, 2 * pairs, own // 2), jnp.bfloat16),
            pltpu.SemaphoreType.DMA((2,)),
            pltpu.SemaphoreType.DMA((owners,)),
            pltpu.SemaphoreType.DMA((owners,)),
            pltpu.SemaphoreType.DMA((owners,)),
            pltpu.SemaphoreType.DMA((owners,)),
            pltpu.SemaphoreType.DMA((groups,)),
            pltpu.SemaphoreType.DMA((groups,)),
            pltpu.SemaphoreType.DMA((groups, groups)),
            pltpu.SemaphoreType.DMA((groups,)),
            pltpu.SemaphoreType.DMA((ratio, groups)),
            pltpu.SemaphoreType.DMA((ratio, groups)),
        ],
        compiler_params=pltpu.CompilerParams(
            collective_id=0, has_side_effects=True, vmem_limit_bytes=60 * 2**20
        ),
        name="gather",
    )(codes, valence_energy, conduction_energy, valence_waves, conduction_waves, first_table, second_table, xtable)

    tile = min(256, own)
    return pl.pallas_call(
        product_kernel,
        grid=(own // tile,),
        out_shape=jax.ShapeDtypeStruct((own, ratio * own), jnp.float32),
        in_specs=[
            pl.BlockSpec((pairs_all, tile), lambda i: (0, i)),
            pl.BlockSpec((pairs_all, ratio * own), lambda i: (0, 0)),
        ],
        out_specs=pl.BlockSpec((tile, ratio * own), lambda i: (i, 0)),
        compiler_params=pltpu.CompilerParams(vmem_limit_bytes=48 * 2**20),
        name="product",
    )(rows, owned)


def solution(mesh):
    in_specs = (P("band", "fft", None, None), P(None, "fft", None, None), P("band"), P(), P("fft"))
    out_specs = P("fft", "band")
    return jax.shard_map(
        on_device, mesh=mesh, in_specs=in_specs, out_specs=out_specs, check_vma=False
    )
```

```python
import functools
import math

import jax
import jax.numpy as jnp
from jax import lax
from jax.experimental import pallas as pl
from jax.experimental.pallas import tpu as pltpu
from jax.sharding import PartitionSpec as P

LANES = 128
MESH = pl.DeviceIdType.MESH


def dft_tables(length):
    counter = jnp.arange(length, dtype=jnp.int32)
    product = counter[:, None] * counter[None, :] % length
    angles = product.astype(jnp.float32) * (2.0 * math.pi / length)
    factor = 1.0 / math.sqrt(length)
    return (
        (jnp.cos(angles) * factor).astype(jnp.bfloat16),
        (jnp.sin(angles) * factor).astype(jnp.bfloat16),
    )


def transform(valence_ref, conduction_ref, first_ref, second_ref, planes, length):
    bands = conduction_ref.shape[0]
    pairs = valence_ref.shape[0] * bands
    slab = valence_ref.shape[1]

    def one_plane(x, carry):
        for v in range(valence_ref.shape[0]):
            density = (valence_ref[v, x][None] * conduction_ref[:, x]).reshape(bands * length, length)
            first = jnp.dot(density, first_ref[...], preferred_element_type=jnp.float32)
            first = first.astype(jnp.bfloat16)
            for c in range(0, bands, 2):
                columns = []
                for d in range(c, c + 2):
                    one = first[d * length : (d + 1) * length]
                    columns.append(jnp.concatenate([one[:, :LANES], one[:, LANES:]], axis=0))
                both = jnp.concatenate(columns, axis=1)
                second = jnp.dot(second_ref[...], both, preferred_element_type=jnp.float32)
                for d in range(2):
                    row = x * pairs + v * bands + c + d
                    planes[pl.ds(row, 2 * length, stride=slab * pairs), :] = second[
                        :, d * LANES : (d + 1) * LANES
                    ]
        return carry

    lax.fori_loop(0, slab, one_plane, 0)


def sample_tile(codes, left, xtable_ref, pairs, slab):
    tile = codes.shape[1]
    depth = left.shape[1]
    kx = codes & 255
    q = (codes >> 8) & (LANES - 1)
    ky = (codes >> 15) & 31
    imag = (codes >> 20) > 0
    hot_q = lax.broadcasted_iota(jnp.int32, (LANES, tile), 0) == q
    hot_q = jnp.where(hot_q, 1.0, 0.0).astype(jnp.bfloat16)
    blocks = []
    for k in range(depth // LANES):
        blocks.append(hot_q * jnp.where(ky == k, 1.0, 0.0).astype(jnp.bfloat16))
    hot = jnp.concatenate(blocks, axis=0)
    picked = jnp.dot(left[...], hot, preferred_element_type=jnp.float32)
    hot_x = lax.broadcasted_iota(jnp.int32, (LANES, tile), 0) == kx
    hot_x = jnp.where(hot_x, 1.0, 0.0).astype(jnp.bfloat16)
    waves = jnp.dot(xtable_ref[...], hot_x, preferred_element_type=jnp.float32)
    half = waves.shape[0] // 2
    cos, sin = waves[:half], waves[half:]
    with_re = jnp.where(imag, -sin, cos)
    with_im = jnp.where(imag, cos, sin)
    total = jnp.zeros((pairs, tile), jnp.float32)
    for x in range(slab):
        re = picked[x * pairs : (x + 1) * pairs]
        im = picked[(slab + x) * pairs : (slab + x + 1) * pairs]
        total += with_re[x : x + 1] * re + with_im[x : x + 1] * im
    return total


def gather_kernel(length, bands_axis, owners, tile, codes_ref, valence_energy, conduction_energy,
                  valence_hbm, conduction_hbm, first_ref, second_ref, xtable_ref, rows_ref, owned_ref,
                  valence_ref, conduction_ref, planes, left, codes_all, work, partial, arrived,
                  row_parts, owned_parts, load_sem,
                  code_send, code_recv, part_send, part_recv, row_send, row_recv, own_send, own_recv,
                  side_send, side_recv):
    pairs = valence_ref.shape[0] * conduction_ref.shape[0]
    slab = valence_ref.shape[1]
    rows = 2 * slab * pairs
    own = codes_ref.shape[1]
    half = own // 2
    yslab = length // owners
    ratio = owned_parts.shape[0]
    band = lax.axis_index("band")
    me = lax.axis_index("fft")
    root = me // ratio
    slot = lax.rem(me, ratio)
    loads = [
        pltpu.make_async_copy(valence_hbm, valence_ref, load_sem.at[0]),
        pltpu.make_async_copy(conduction_hbm, conduction_ref, load_sem.at[1]),
    ]
    for load in loads:
        load.start()

    def around(shift):
        return lax.rem(me + shift, owners)

    def across(shift):
        return lax.rem(band + shift, bands_axis)

    barrier = pltpu.get_barrier_semaphore()

    def greet_fft(shift, carry):
        pl.semaphore_signal(barrier, inc=1, device_id=(band, around(shift)), device_id_type=MESH)
        return carry

    def greet_band(shift, carry):
        pl.semaphore_signal(barrier, inc=1, device_id=(across(shift), me), device_id_type=MESH)
        return carry

    lax.fori_loop(1, owners, greet_fft, 0)
    lax.fori_loop(1, bands_axis, greet_band, 0)
    pl.semaphore_wait(barrier, owners + bands_axis - 2)

    def code_copy(shift):
        return pltpu.make_async_remote_copy(
            src_ref=codes_ref, dst_ref=codes_all.at[shift],
            send_sem=code_send.at[shift], recv_sem=code_recv.at[shift],
            device_id=(band, around(shift)), device_id_type=MESH,
        )

    def part_copy(shift):
        return pltpu.make_async_remote_copy(
            src_ref=partial.at[shift], dst_ref=arrived.at[shift],
            send_sem=part_send.at[shift], recv_sem=part_recv.at[shift],
            device_id=(band, around(owners - shift)), device_id_type=MESH,
        )

    def row_copy(shift):
        return pltpu.make_async_remote_copy(
            src_ref=row_parts.at[band], dst_ref=row_parts.at[band],
            send_sem=row_send.at[shift], recv_sem=row_recv.at[shift],
            device_id=(across(shift), me), device_id_type=MESH,
        )

    def row_wait(shift):
        source = across(bands_axis - shift)
        return pltpu.make_async_remote_copy(
            src_ref=row_parts.at[band], dst_ref=row_parts.at[source],
            send_sem=row_send.at[shift], recv_sem=row_recv.at[shift],
            device_id=(across(shift), me), device_id_type=MESH,
        )

    def owned_copy(hop, shift):
        chunk = across(bands_axis - shift)
        return pltpu.make_async_remote_copy(
            src_ref=owned_parts.at[slot, chunk], dst_ref=owned_parts.at[slot, chunk],
            send_sem=own_send.at[hop, shift], recv_sem=own_recv.at[shift],
            device_id=(band, across(hop) * ratio + slot), device_id_type=MESH,
        )

    def side_copy(hop, shift, source):
        chunk = across(bands_axis - shift)
        return pltpu.make_async_remote_copy(
            src_ref=owned_parts.at[source, chunk], dst_ref=owned_parts.at[source, chunk],
            send_sem=side_send.at[hop, shift], recv_sem=side_recv.at[hop, shift],
            device_id=(band, root * ratio + lax.rem(slot + hop, ratio)), device_id_type=MESH,
        )

    def each(first, last, act):
        def step(i, carry):
            act(i)
            return carry

        lax.fori_loop(first, last, step, 0)

    each(1, owners, lambda s: code_copy(s).start())
    codes_all[0] = codes_ref[...]
    for load in loads:
        load.wait()
    transform(valence_ref, conduction_ref, first_ref, second_ref, planes, length)

    def folded(array):
        return jnp.concatenate([array[:, :half], array[:, half:]], axis=0)

    def one_owner(step):
        shift = lax.rem(step, owners)
        o = lax.rem(me + owners - shift, owners)

        @pl.when(shift > 0)
        def _():
            code_copy(shift).wait_recv()

        for k in range(yslab):
            part = planes[pl.ds(pl.multiple_of((o * yslab + k) * rows, rows), rows), :]
            left[:, k * LANES : (k + 1) * LANES] = part.astype(jnp.bfloat16)

        for t in range(0, own, tile):
            codes = codes_all[shift, :, t : t + tile]
            work[:, t : t + tile] = sample_tile(codes, left, xtable_ref, pairs, slab)

        @pl.when(shift > 0)
        def _():
            partial[shift] = folded(work).astype(jnp.bfloat16)
            part_copy(shift).start()

    each(1, owners + 1, one_owner)
    each(1, owners, lambda s: code_copy(s).wait_send())

    line = lax.broadcasted_iota(jnp.int32, (2 * pairs, LANES), 0)
    spacing = jnp.ones((2 * pairs, LANES), jnp.float32)
    bands = conduction_ref.shape[0]
    for p in range(2 * pairs):
        v, c = p % pairs // bands, p % bands
        spacing = jnp.where(line == p, conduction_energy[c] - valence_energy[v], spacing)
    factor = jnp.sqrt(4.0 / (spacing * (bands_axis * pairs)))

    total = folded(work)
    for s in range(1, owners):
        part_copy(s).wait_recv()
        total += arrived[s].astype(jnp.float32)
    row_parts[band] = (factor[:, :1] * total).astype(jnp.bfloat16)
    each(1, bands_axis, lambda s: row_copy(s).start())
    mine = root == band

    def one_chunk(shift):
        chunk = across(bands_axis - shift)

        @pl.when(shift > 0)
        def _():
            row_wait(shift).wait_recv()

        @pl.when(mine)
        def _():
            owned_parts[slot, chunk] = row_parts[chunk]
            each(1, bands_axis, lambda hop: owned_copy(hop, shift).start())

        @pl.when(jnp.logical_not(mine))
        def _():
            owned_copy(0, shift).wait_recv()

        for hop in range(1, ratio):
            side_copy(hop, shift, slot).start()

    each(0, bands_axis, one_chunk)

    def join(parts):
        parts = parts.astype(jnp.float32)
        halves = [parts[:, h * pairs : (h + 1) * pairs].reshape(bands_axis * pairs, half) for h in range(2)]
        return jnp.concatenate(halves, axis=1)

    rows_ref[...] = join(row_parts[...]).astype(jnp.bfloat16)
    for hop in range(1, ratio):
        source = lax.rem(slot + ratio - hop, ratio)
        each(0, bands_axis, lambda s: side_copy(hop, s, source).wait_recv())
    for j in range(ratio):
        owned_ref[:, j * own : (j + 1) * own] = (-join(owned_parts[j])).astype(jnp.bfloat16)

    each(1, owners, lambda s: part_copy(s).wait_send())
    each(1, bands_axis, lambda s: row_copy(s).wait_send())

    @pl.when(mine)
    def _():
        each(0, bands_axis, lambda s: each(1, bands_axis, lambda hop: owned_copy(hop, s).wait_send()))

    for hop in range(1, ratio):
        each(0, bands_axis, lambda s: side_copy(hop, s, slot).wait_send())


def product_kernel(rows_ref, owned_ref, out_ref):
    contract = (((0,), (0,)), ((), ()))
    out_ref[...] = lax.dot_general(
        rows_ref[...], owned_ref[...], contract, preferred_element_type=jnp.float32
    )


def on_device(valence_waves, conduction_waves, valence_energy, conduction_energy, sphere_slots):
    length = conduction_waves.shape[2]
    bands = conduction_waves.shape[0]
    slab = conduction_waves.shape[1]
    groups = lax.axis_size("band")
    owners = lax.axis_size("fft")
    pairs = valence_waves.shape[0] * bands
    pairs_all = groups * pairs
    own = sphere_slots.shape[0]
    yslab = length // owners
    ratio = owners // groups
    me = lax.axis_index("fft")

    table_cos, table_sin = dft_tables(length)
    gap = ((0, 0), (0, LANES - length))
    first_table = jnp.concatenate([jnp.pad(table_cos, gap), jnp.pad(-table_sin, gap)], axis=1)
    second_table = jnp.stack(
        [
            jnp.concatenate([table_cos, table_sin], axis=1),
            jnp.concatenate([-table_sin, table_cos], axis=1),
        ],
        axis=1,
    ).reshape(2 * length, 2 * length)
    short = -slab % 16
    pieces = []
    for table in (table_cos, table_sin):
        piece = lax.dynamic_slice_in_dim(table, me * slab, slab, axis=0)
        pieces.append(jnp.pad(piece, ((0, short), (0, LANES - length))))
    xtable = jnp.concatenate(pieces, axis=0)

    width = 2 * length
    kx = sphere_slots // (yslab * width)
    ky = (sphere_slots // width) % yslab
    comp = sphere_slots % width
    imag = (comp >= length).astype(jnp.int32)
    codes = (kx + ((ky * LANES + comp - imag * length) << 8) + (imag << 20))[None]
    rows, owned = pl.pallas_call(
        functools.partial(gather_kernel, length, groups, owners, min(512, own)),
        out_shape=(
            jax.ShapeDtypeStruct((pairs_all, own), jnp.bfloat16),
            jax.ShapeDtypeStruct((pairs_all, ratio * own), jnp.bfloat16),
        ),
        in_specs=[pl.BlockSpec(memory_space=pltpu.VMEM)]
        + [pl.BlockSpec(memory_space=pltpu.SMEM)] * 2
        + [pl.BlockSpec(memory_space=pl.ANY)] * 2
        + [pl.BlockSpec(memory_space=pltpu.VMEM)] * 3,
        out_specs=(pl.BlockSpec(memory_space=pltpu.VMEM), pl.BlockSpec(memory_space=pltpu.VMEM)),
        scratch_shapes=[
            pltpu.VMEM(valence_waves.shape, jnp.bfloat16),
            pltpu.VMEM(conduction_waves.shape, jnp.bfloat16),
            pltpu.VMEM((2 * length * slab * pairs, LANES), jnp.float32),
            pltpu.VMEM((2 * slab * pairs, yslab * LANES), jnp.bfloat16),
            pltpu.VMEM((owners, 1, own), jnp.int32),
            pltpu.VMEM((pairs, own), jnp.float32),
            pltpu.VMEM((owners, 2 * pairs, own // 2), jnp.bfloat16),
            pltpu.VMEM((owners, 2 * pairs, own // 2), jnp.bfloat16),
            pltpu.VMEM((groups, 2 * pairs, own // 2), jnp.bfloat16),
            pltpu.VMEM((ratio, groups, 2 * pairs, own // 2), jnp.bfloat16),
            pltpu.SemaphoreType.DMA((2,)),
            pltpu.SemaphoreType.DMA((owners,)),
            pltpu.SemaphoreType.DMA((owners,)),
            pltpu.SemaphoreType.DMA((owners,)),
            pltpu.SemaphoreType.DMA((owners,)),
            pltpu.SemaphoreType.DMA((groups,)),
            pltpu.SemaphoreType.DMA((groups,)),
            pltpu.SemaphoreType.DMA((groups, groups)),
            pltpu.SemaphoreType.DMA((groups,)),
            pltpu.SemaphoreType.DMA((ratio, groups)),
            pltpu.SemaphoreType.DMA((ratio, groups)),
        ],
        compiler_params=pltpu.CompilerParams(
            collective_id=0, has_side_effects=True, vmem_limit_bytes=119 * 2**19
        ),
        name="gather",
    )(codes, valence_energy, conduction_energy, valence_waves, conduction_waves, first_table, second_table, xtable)

    tile = min(256, own)
    return pl.pallas_call(
        product_kernel,
        grid=(own // tile,),
        out_shape=jax.ShapeDtypeStruct((own, ratio * own), jnp.float32),
        in_specs=[
            pl.BlockSpec((pairs_all, tile), lambda i: (0, i)),
            pl.BlockSpec((pairs_all, ratio * own), lambda i: (0, 0)),
        ],
        out_specs=pl.BlockSpec((tile, ratio * own), lambda i: (i, 0)),
        compiler_params=pltpu.CompilerParams(vmem_limit_bytes=48 * 2**20),
        name="product",
    )(rows, owned)


def solution(mesh):
    in_specs = (P("band", "fft", None, None), P(None, "fft", None, None), P("band"), P(), P("fft"))
    out_specs = P("fft", "band")
    return jax.shard_map(
        on_device, mesh=mesh, in_specs=in_specs, out_specs=out_specs, check_vma=False
    )
```
